256 devices in a mesh: row: 16 (over y, x), col: 8 (over z), vox: 2 (over core).
Axes of the slice: x: 4, y: 4, z: 8, core: 2. Of those that a mesh axis runs over, the one named last changes fastest.
Arguments:
- coeffs_r: bfloat16 [32, 16, 64, 2, 1024], P(None, 'row', None, None, 'col'), may hold values from -0.125 to 0.125
- rhs: bfloat16 [32, 16, 64, 1536], P('col', 'row', None, 'vox'), may hold values from -6 to 6
- inverses: bfloat16 [2, 1024, 1024], replicated, may hold values from -0.1875 to 0.1875
Outputs:
- updated: bfloat16 [32, 16, 64, 1536], P('col', 'row', None, 'vox')
The draws below stay inside these ranges and needn't reach their ends.
All inputs are finite; a program needn't handle non-finite values.
Results may differ from the reference program's by a relative error of at most 0.0049.
Values may be sent and summed in bfloat16 or wider, within the bound.
A program may use at most 64 MiB of HBM per device.

```python
import jax
import jax.numpy as jnp

NB = 1024
VOX = 1536
RB = 64
RGRID = 16
CYC = 32


def level_of(rng, dims, pieces, smallest, high):
    def one(position, shards_of):
        heights = jax.random.uniform(jax.random.fold_in(jax.random.fold_in(rng, 6), position), (shards_of,), jnp.float32, smallest / len(pieces), high / len(pieces))
        return jnp.repeat(jnp.exp(heights), dims[position] // shards_of).reshape((-1,) + (1,) * (len(dims) - position - 1))

    gain = one(*pieces[0])
    for cut in pieces[1:]:
        gain = gain * one(*cut)
    return gain


def scatter_about(own_key, dims, spread, reach, shards=(), held_as=jnp.bfloat16):
    loudness = level_of(own_key, dims, shards, -0.22, 0.18) if shards else 1.0
    result = jax.random.normal(own_key, dims, jnp.float32) * spread * loudness
    return jnp.minimum(jnp.maximum(result, -reach), reach).astype(held_as)


def setup_inputs(seed: int = 0) -> dict:
    splits = jax.random.split(jax.random.key(seed), 4)
    coeffs_r = scatter_about(splits[0], (CYC, RGRID, RB, 2, NB), (2 * NB) ** -0.5, 0.125, ((1, 16), (4, 8)))
    rhs = scatter_about(splits[1], (CYC, RGRID, RB, VOX), 1.0, 6.0, ((0, 8), (1, 16), (3, 2)))
    inverses = scatter_about(splits[2], (2, NB, NB), NB ** -0.5, 0.1875)
    return dict(coeffs_r=coeffs_r, rhs=rhs, inverses=inverses)


def reference(coeffs_r, rhs, inverses):
    order = CYC * RGRID * RB
    factor = coeffs_r.reshape(order, 2, NB)
    right = rhs.reshape(order, VOX)
    top = order - 2 * NB
    x_last = jnp.dot(inverses[1], right[order - NB:], preferred_element_type=jnp.float32).astype(jnp.bfloat16)
    mid_rhs = right[top:order - NB].astype(jnp.float32) - jnp.dot(factor[top:order - NB, 1], x_last, preferred_element_type=jnp.float32)
    mid_rhs = mid_rhs.astype(jnp.bfloat16)
    x_mid = jnp.dot(inverses[0], mid_rhs, preferred_element_type=jnp.float32).astype(jnp.bfloat16)
    remaining = right[:top].astype(jnp.float32) - jnp.dot(factor[:top, 0], x_mid, preferred_element_type=jnp.float32)
    remaining = remaining - jnp.dot(factor[:top, 1], x_last, preferred_element_type=jnp.float32)
    joined = jnp.concatenate([remaining.astype(jnp.bfloat16), x_mid, x_last], 0)
    return joined.reshape(CYC, RGRID, RB, VOX)
```

```python
import jax
import jax.numpy as jnp
from jax import lax
from jax.experimental import pallas as pl
from jax.experimental.pallas import tpu as pltpu
from jax.sharding import PartitionSpec as P

MESH = pl.DeviceIdType.MESH
BF = jnp.bfloat16
F32 = jnp.float32
X, Y, Z = 4, 4, 8
CHUNKS, WIDTH = 3, 256
ROWS = 64
HALF = ROWS // 2
OWN = 128
ORDER = 1024
LAST = Z - 1


def dot(a, b):
    return jnp.dot(a, b, preferred_element_type=F32)


def split_pairs():
    r = lax.broadcasted_iota(jnp.int32, (2 * ROWS, 2 * ROWS), 0)
    c = lax.broadcasted_iota(jnp.int32, (2 * ROWS, 2 * ROWS), 1)
    wanted = jnp.where(r < ROWS, 2 * r, 2 * (r - ROWS) + 1)
    return jnp.where(c == wanted, 1.0, 0.0).astype(BF)


def kernel(
    coeffs,
    rhs,
    inverses,
    out,
    inv,
    mine,
    paired,
    mid_raw,
    factor,
    panel,
    known,
    tail,
    middle,
    solved_last,
    solved_mid,
    acc,
    local_sem,
    z_send,
    z_recv,
    k_send,
    k_recv,
    p_send,
    p_recv,
    c_send,
    c_recv,
    s_send,
    s_recv,
    g_send,
    g_recv,
):
    row = lax.axis_index("row")
    z = lax.axis_index("col")
    core = lax.axis_index("vox")
    x, y = lax.rem(row, X), row // X

    def at_z(d):
        return (row, lax.rem(z + d, Z), core)

    def at_x(d):
        return (y * X + lax.rem(x + d, X), z, core)

    def at_y(d):
        return (lax.rem(y + d, Y) * X + x, z, core)

    sibling = (row, z, 1 - core)

    def remote(src, dst, send, recv, where):
        return pltpu.make_async_remote_copy(
            src_ref=src, dst_ref=dst, send_sem=send, recv_sem=recv, device_id=where, device_id_type=MESH
        )

    def columns(j):
        return pl.ds(j * WIDTH, WIDTH)

    load_rhs = pltpu.make_async_copy(rhs, mine, local_sem.at[0])
    load_mid = pltpu.make_async_copy(coeffs.at[30], mid_raw, local_sem.at[1])
    load_inv1 = pltpu.make_async_copy(inverses.at[1], inv.at[1], local_sem.at[2])
    load_own = pltpu.make_async_copy(coeffs.at[pl.ds(4 * z, 4)], paired.at[z], local_sem.at[3])
    load_inv0 = pltpu.make_async_copy(inverses.at[0], inv.at[0], local_sem.at[4])
    for load in (load_rhs, load_mid, load_inv1, load_own, load_inv0):
        load.start()

    barrier = pltpu.get_barrier_semaphore()
    peers = [at_z(d) for d in range(1, Z)] + [at_x(d) for d in range(1, X)] + [at_y(d) for d in range(1, Y)] + [sibling]
    for peer in peers:
        pl.semaphore_signal(barrier, inc=1, device_id=peer, device_id_type=MESH)
    load_rhs.wait()
    load_mid.wait()
    pick = split_pairs()
    panel_mine = dot(pick[ROWS:], mid_raw[...]).astype(BF)
    panel[z] = panel_mine
    pl.semaphore_wait(barrier, len(peers))

    def tail_copy(j, d):
        return remote(mine.at[3, :, columns(j)], tail.at[j, y, x], z_send.at[j, d - 1], z_recv.at[j], at_z(d))

    def known_copy(d):
        return remote(mine.at[2], known, k_send.at[d - 1], k_recv, at_z(d))

    def panel_copy(d):
        return remote(panel.at[z], panel.at[z], p_send.at[d - 1], p_recv.at[d - 1], at_z(d))

    order = (4, 3, 5, 2, 6, 1, 7)

    @pl.when(z == LAST)
    def _():
        for d in order:
            tail_copy(0, d).start()

    for d in order:
        panel_copy(d).start()

    @pl.when(z == LAST)
    def _():
        for j in range(1, CHUNKS):
            for d in order:
                tail_copy(j, d).start()
        for d in order:
            known_copy(d).start()
        for j in range(CHUNKS):
            tail[j, y, x] = mine[3, :, j * WIDTH : (j + 1) * WIDTH]
        known[...] = mine[2]

    upper, lower = pl.ds(0, HALF), pl.ds(HALF, HALF)

    def gather(which, buf, j, stage, half, d):
        send, recv = g_send.at[which, j, stage, half, d - 1], g_recv.at[which, j, stage, half, d - 1]
        if stage == 0:
            rows = upper if half == 0 else lower
            part, where = buf.at[j, y, x, rows], (at_x(d) if half == 0 else at_y(d))
        elif half == 0:
            part, where = buf.at[j, y, :, upper], at_y(d)
        else:
            part, where = buf.at[j, :, x, lower], at_x(d)
        return remote(part, part, send, recv, where)

    every = [(half, d) for d in (2, 1, 3) for half in (0, 1)]

    def start(which, buf, j, stage):
        for half, d in every:
            gather(which, buf, j, stage, half, d).start()

    def arrive(which, buf, j, stage):
        for half, d in every:
            gather(which, buf, j, stage, half, d).wait_recv()

    def tail_here(j):
        @pl.when(z != LAST)
        def _():
            tail_copy(j, 1).wait_recv()

        start(0, tail, j, 0)

    def coeff_copy(d):
        to = lax.rem(z + d, Z)
        return remote(
            coeffs.at[pl.ds(4 * to + 2 * core, 2)],
            paired.at[z, pl.ds(2 * core, 2)],
            c_send.at[d - 1],
            c_recv.at[d - 1],
            at_z(d),
        )

    def share_copy(d):
        part = paired.at[lax.rem(z + Z - d, Z), pl.ds(2 * core, 2)]
        return remote(part, part, s_send.at[d - 1], s_recv.at[d - 1], sibling)

    tail_here(0)
    tail_here(1)
    arrive(0, tail, 0, 0)
    start(0, tail, 0, 1)
    tail_here(2)
    for d in order:
        coeff_copy(d).start()
    arrive(0, tail, 1, 0)
    start(0, tail, 1, 1)
    arrive(0, tail, 2, 0)
    start(0, tail, 2, 1)

    load_inv1.wait()
    for d in order:
        panel_copy(d).wait_recv()

    @pl.when(z != LAST)
    def _():
        known_copy(1).wait_recv()

    panel_full = jnp.concatenate([panel[c] for c in range(Z)], axis=1)

    def solve_last(j):
        arrive(0, tail, j, 1)
        block = tail[j].reshape(ORDER, WIDTH)
        solved = dot(inv[1], block).astype(BF)
        solved_last[j] = solved
        part = known[:, j * WIDTH : (j + 1) * WIDTH].astype(F32) - dot(panel_full, solved)
        middle[j, y, x] = part.astype(BF)
        start(1, middle, j, 0)

    def pass_on(j):
        arrive(1, middle, j, 0)
        start(1, middle, j, 1)

    solve_last(0)
    solve_last(1)
    pass_on(0)
    solve_last(2)
    pass_on(1)
    for d in order:
        coeff_copy(d).wait_recv()
        share_copy(d).start()
    pass_on(2)
    load_own.wait()
    load_inv0.wait()
    for d in order:
        share_copy(d).wait_recv()
    for k in range(4):
        both = dot(pick, jnp.concatenate([paired[c, k] for c in range(Z)], axis=1)).astype(BF)
        factor[0, k * ROWS : (k + 1) * ROWS] = both[:ROWS]
        factor[1, k * ROWS : (k + 1) * ROWS] = both[ROWS:]
    for j in range(CHUNKS):
        here = mine[:, :, j * WIDTH : (j + 1) * WIDTH].reshape(4 * ROWS, WIDTH).astype(F32)
        acc[j] = here - dot(factor[1], solved_last[j])
    own_rows = pl.ds(pl.multiple_of(row * ROWS, ROWS), ROWS)
    for j in range(CHUNKS):
        arrive(1, middle, j, 1)
        solved = dot(inv[0], middle[j].reshape(ORDER, WIDTH)).astype(BF)
        solved_mid[...] = solved
        result = (acc[j] - dot(factor[0], solved)).astype(BF)
        out[:, :, j * WIDTH : (j + 1) * WIDTH] = result.reshape(4, ROWS, WIDTH)

        @pl.when(z == LAST)
        def _():
            out[2, :, j * WIDTH : (j + 1) * WIDTH] = solved_mid[own_rows]
            out[3, :, j * WIDTH : (j + 1) * WIDTH] = solved_last[j, own_rows]

    @pl.when(z == LAST)
    def _():
        for d in order:
            for j in range(CHUNKS):
                tail_copy(j, d).wait_send()
            known_copy(d).wait_send()

    for d in order:
        panel_copy(d).wait_send()
        coeff_copy(d).wait_send()
        share_copy(d).wait_send()
    for which, buf in ((0, tail), (1, middle)):
        for j in range(CHUNKS):
            for stage in range(2):
                for half, d in every:
                    gather(which, buf, j, stage, half, d).wait_send()


def local(coeffs_r, rhs, inverses):
    cycles = coeffs_r.shape[0]
    any_space = pl.BlockSpec(memory_space=pl.ANY)
    dma = pltpu.SemaphoreType.DMA
    out = pl.pallas_call(
        kernel,
        out_shape=jax.ShapeDtypeStruct((4, ROWS, CHUNKS * WIDTH), BF),
        in_specs=[any_space] * 3,
        out_specs=pl.BlockSpec(memory_space=pltpu.VMEM),
        scratch_shapes=[
            pltpu.VMEM((2, ORDER, ORDER), BF),
            pltpu.VMEM((4, ROWS, CHUNKS * WIDTH), BF),
            pltpu.VMEM((Z, 4, 2 * ROWS, OWN), BF),
            pltpu.VMEM((2 * ROWS, OWN), BF),
            pltpu.VMEM((2, 4 * ROWS, ORDER), BF),
            pltpu.VMEM((Z, ROWS, OWN), BF),
            pltpu.VMEM((ROWS, CHUNKS * WIDTH), BF),
            pltpu.VMEM((CHUNKS, Y, X, ROWS, WIDTH), BF),
            pltpu.VMEM((CHUNKS, Y, X, ROWS, WIDTH), BF),
            pltpu.VMEM((CHUNKS, ORDER, WIDTH), BF),
            pltpu.VMEM((ORDER, WIDTH), BF),
            pltpu.VMEM((CHUNKS, 4 * ROWS, WIDTH), F32),
            dma((5,)),
            dma((CHUNKS, Z - 1)),
            dma((CHUNKS,)),
            dma((Z - 1,)),
            dma,
            dma((Z - 1,)),
            dma((Z - 1,)),
            dma((Z - 1,)),
            dma((Z - 1,)),
            dma((Z - 1,)),
            dma((Z - 1,)),
            dma((2, CHUNKS, 2, 2, 3)),
            dma((2, CHUNKS, 2, 2, 3)),
        ],
        compiler_params=pltpu.CompilerParams(
            collective_id=0, has_side_effects=True, vmem_limit_bytes=60 * 1024 * 1024
        ),
    )(
        coeffs_r.reshape(cycles, 2 * ROWS, OWN),
        rhs.reshape(4, ROWS, CHUNKS * WIDTH),
        inverses,
    )
    return out.reshape(rhs.shape)


def solution(mesh):
    placed = (P(None, "row", None, None, "col"), P("col", "row", None, "vox"), P())
    return jax.shard_map(
        local, mesh=mesh, in_specs=placed, out_specs=P("col", "row", None, "vox"), check_vma=False
    )
```

```python
import jax
import jax.numpy as jnp
from jax import lax
from jax.experimental import pallas as pl
from jax.experimental.pallas import tpu as pltpu
from jax.sharding import PartitionSpec as P

MESH = pl.DeviceIdType.MESH
BF = jnp.bfloat16
F32 = jnp.float32
X, Y, Z = 4, 4, 8
SIDE = 384
WIDTHS = (256, 128)
STARTS = (0, 256)
CHUNKS = len(WIDTHS)
ROWS = 64
HALF = ROWS // 2
OWN = 128
ORDER = 1024
LAST = Z - 1
FAR_FIRST = (4, 3, 5, 2, 6, 1, 7)


def dot(a, b):
    return jnp.dot(a, b, preferred_element_type=F32)


def picker(rows, wanted):
    r = lax.broadcasted_iota(jnp.int32, (rows, 2 * ROWS), 0)
    c = lax.broadcasted_iota(jnp.int32, (rows, 2 * ROWS), 1)
    return jnp.where(c == wanted(r), 1.0, 0.0).astype(BF)


def kernel(
    coeffs,
    rhs,
    inverses,
    out,
    inv,
    here,
    paired,
    mid_raw,
    factor,
    panel,
    known,
    tail0,
    tail1,
    middle0,
    middle1,
    last0,
    last1,
    solved0,
    solved1,
    acc0,
    acc1,
    res0,
    res1,
    local_sem,
    out_sem,
    t_send,
    t_recv,
    k_send,
    k_recv,
    h_send,
    h_recv,
    p_send,
    p_recv,
    q_send,
    q_recv,
    r_send,
    r_recv,
    s_send,
    s_recv,
    g_send,
    g_recv,
    o_send,
    o_recv,
):
    row = lax.axis_index("row")
    z = lax.axis_index("col")
    core = lax.axis_index("vox")
    x, y = lax.rem(row, X), row // X
    odd = lax.rem(z, 2)
    toward = 1 - 2 * odd
    tail, middle, last = (tail0, tail1), (middle0, middle1), (last0, last1)
    solved_mid, acc, res = (solved0, solved1), (acc0, acc1), (res0, res1)

    def turn(d):
        return lax.rem(z + 2 * Z + d, Z)

    def at_z(d):
        return (row, turn(d), core)

    def at_x(d):
        return (y * X + lax.rem(x + d, X), z, core)

    def at_y(d):
        return (lax.rem(y + d, Y) * X + x, z, core)

    partner = at_z(toward)
    sibling = (row, z, 1 - core)

    def remote(src, dst, send, recv, where):
        return pltpu.make_async_remote_copy(
            src_ref=src, dst_ref=dst, send_sem=send, recv_sem=recv, device_id=where, device_id_type=MESH
        )

    def side(h, j):
        return pl.ds(h * SIDE + STARTS[j], WIDTHS[j])

    my_side = pl.ds(pl.multiple_of(odd * SIDE, OWN), SIDE)
    other_side = pl.ds(pl.multiple_of((1 - odd) * SIDE, OWN), SIDE)
    pair_cycles = 8 * (z // 2)

    load_mid = pltpu.make_async_copy(coeffs.at[30], mid_raw, local_sem.at[0])
    load_inv1 = pltpu.make_async_copy(inverses.at[1], inv.at[1], local_sem.at[1])
    load_own = pltpu.make_async_copy(coeffs.at[pl.ds(pair_cycles, 8)], paired.at[z], local_sem.at[2])
    load_here = pltpu.make_async_copy(rhs.at[:, :, my_side], here.at[odd], local_sem.at[3])
    load_inv0 = pltpu.make_async_copy(inverses.at[0], inv.at[0], local_sem.at[4])
    load_tail = [
        pltpu.make_async_copy(rhs.at[3, :, side(1, j)], tail[j].at[y, x], local_sem.at[5 + j]) for j in range(CHUNKS)
    ]
    load_known = pltpu.make_async_copy(rhs.at[2, :, pl.ds(SIDE, SIDE)], known, local_sem.at[5 + CHUNKS])

    barrier = pltpu.get_barrier_semaphore()
    peers = [at_z(d) for d in range(1, Z)] + [at_x(d) for d in range(1, X)] + [at_y(d) for d in range(1, Y)] + [sibling]
    for peer in peers:
        pl.semaphore_signal(barrier, inc=1, device_id=peer, device_id_type=MESH)
    load_mid.start()

    @pl.when(z == LAST)
    def _():
        for load in (*load_tail, load_known):
            load.start()

    for load in (load_inv1, load_own, load_here, load_inv0):
        load.start()
    load_mid.wait()
    panel[core, z] = dot(picker(HALF, lambda r: 2 * (r + HALF * core) + 1), mid_raw[...]).astype(BF)
    pl.semaphore_wait(barrier, len(peers))

    def tail_copy(j, d):
        return remote(rhs.at[3, :, side((d - 1) % 2, j)], tail[j].at[y, x], t_send.at[j, d - 1], t_recv.at[j], at_z(d))

    def known_copy(d):
        return remote(rhs.at[2, :, pl.ds((d - 1) % 2 * SIDE, SIDE)], known, k_send.at[d - 1], k_recv, at_z(d))

    def here_copy():
        return remote(rhs.at[:, :, other_side], here.at[odd], h_send, h_recv, partner)

    def panel_copy(d):
        part = panel.at[core, z]
        return remote(part, part, p_send.at[d - 1], p_recv.at[d - 1], at_z(d))

    def panel_share():
        return remote(panel.at[core], panel.at[core], q_send, q_recv, sibling)

    four = pl.ds(4 * core, 4)

    def factor_copy(k):
        shift = {1: -toward, 2: 2 * toward, 3: -3 * toward, 4: toward}[k]
        source = coeffs.at[pl.ds(8 * (turn(shift) // 2) + 4 * core, 4)]
        return remote(source, paired.at[z, four], r_send.at[k - 1], r_recv.at[k - 1], at_z(shift))

    def pass_copy(k):
        part = paired.at[turn(-k * toward), four]
        return remote(part, part, r_send.at[3 + k], r_recv.at[3 + k], partner)

    def share_copy(k):
        part = paired.at[turn(-k * toward if k < 4 else (k - 3) * toward), four]
        return remote(part, part, s_send.at[k - 1], s_recv.at[k - 1], sibling)

    @pl.when(z == LAST)
    def _():
        for j in range(CHUNKS):
            for d in FAR_FIRST:
                tail_copy(j, d).start()

    for d in FAR_FIRST:
        panel_copy(d).start()

    @pl.when(z == LAST)
    def _():
        for d in FAR_FIRST:
            known_copy(d).start()
        for load in (*load_tail, load_known):
            load.wait()

    for k in (4, 1, 2, 3):
        factor_copy(k).start()

    upper, lower = pl.ds(0, HALF), pl.ds(HALF, HALF)

    def gather(which, j, stage, half, d):
        buf = (tail, middle)[which][j]
        send, recv = g_send.at[which, j, stage, half, d - 1], g_recv.at[which, j, stage, half, d - 1]
        if stage == 0:
            part, where = buf.at[y, x, upper if half == 0 else lower], (at_x(d) if half == 0 else at_y(d))
        elif half == 0:
            part, where = buf.at[y, :, upper], at_y(d)
        else:
            part, where = buf.at[:, x, lower], at_x(d)
        return remote(part, part, send, recv, where)

    every = [(half, d) for d in (2, 1, 3) for half in (0, 1)]

    def start(which, j, stage):
        for half, d in every:
            gather(which, j, stage, half, d).start()

    def arrive(which, j, stage):
        for half, d in every:
            gather(which, j, stage, half, d).wait_recv()

    def step(which, j):
        arrive(which, j, 0)
        start(which, j, 1)

    for j in range(CHUNKS):

        @pl.when(z != LAST)
        def _():
            tail_copy(j, 1).wait_recv()

        start(0, j, 0)
    here_copy().start()
    step(0, 0)
    step(0, 1)

    def relay(k):
        factor_copy(k).wait_recv()
        pass_copy(k).start()
        share_copy(k).start()

    for d in FAR_FIRST:
        panel_copy(d).wait_recv()
    panel_share().start()
    load_inv1.wait()

    @pl.when(z != LAST)
    def _():
        known_copy(1).wait_recv()

    panel_share().wait_recv()
    panel_full = jnp.concatenate(
        [jnp.concatenate([panel[v, c] for c in range(Z)], axis=1) for v in range(2)], axis=0
    )

    def solve_last(j):
        arrive(0, j, 1)
        solved = dot(inv[1], tail[j][...].reshape(ORDER, WIDTHS[j])).astype(BF)
        last[j][...] = solved
        part = known[:, STARTS[j] : STARTS[j] + WIDTHS[j]].astype(F32) - dot(panel_full, solved)
        middle[j][y, x] = part.astype(BF)
        start(1, j, 0)

    solve_last(0)
    solve_last(1)
    for k in (1, 2, 3):
        relay(k)
    factor_copy(4).wait_recv()
    share_copy(4).start()
    step(1, 0)
    step(1, 1)
    for k in (1, 2, 3):
        pass_copy(k).wait_recv()
        share_copy(4 + k).start()
    load_own.wait()
    load_here.wait()
    here_copy().wait_recv()
    load_inv0.wait()
    for k in range(1, 8):
        share_copy(k).wait_recv()
    pick = picker(2 * ROWS, lambda r: jnp.where(r < ROWS, 2 * r, 2 * (r - ROWS) + 1))
    for k in range(8):
        both = dot(pick, jnp.concatenate([paired[c, k] for c in range(Z)], axis=1)).astype(BF)
        factor[0, k * ROWS : (k + 1) * ROWS] = both[:ROWS]
        factor[1, k * ROWS : (k + 1) * ROWS] = both[ROWS:]
    for j in range(CHUNKS):
        right = here[:, :, :, STARTS[j] : STARTS[j] + WIDTHS[j]].reshape(8 * ROWS, WIDTHS[j]).astype(F32)
        acc[j][...] = right - dot(factor[1], last[j][...])

    own_rows = pl.ds(pl.multiple_of(row * ROWS, ROWS), ROWS)

    def result_place(j):
        return out.at[:, :, pl.ds(pl.multiple_of(odd * SIDE + STARTS[j], OWN), WIDTHS[j])]

    def keep_copy(j):
        return pltpu.make_async_copy(res[j].at[odd], result_place(j), out_sem.at[j])

    def return_copy(j):
        return remote(res[j].at[1 - odd], result_place(j), o_send.at[j], o_recv.at[j], partner)

    for j in range(CHUNKS):
        arrive(1, j, 1)
        solved = dot(inv[0], middle[j][...].reshape(ORDER, WIDTHS[j])).astype(BF)
        solved_mid[j][...] = solved
        result = (acc[j][...] - dot(factor[0], solved)).astype(BF)
        res[j][...] = result.reshape(2, 4, ROWS, WIDTHS[j])

        @pl.when(z >= LAST - 1)
        def _():
            res[j][1, 2] = solved_mid[j][own_rows]
            res[j][1, 3] = last[j][own_rows]

        return_copy(j).start()
        keep_copy(j).start()

    @pl.when(z == LAST)
    def _():
        for d in FAR_FIRST:
            for j in range(CHUNKS):
                tail_copy(j, d).wait_send()
            known_copy(d).wait_send()

    for d in FAR_FIRST:
        panel_copy(d).wait_send()
    panel_share().wait_send()
    here_copy().wait_send()
    for k in range(1, 8):
        share_copy(k).wait_send()
    for k in range(1, 5):
        factor_copy(k).wait_send()
    for k in range(1, 4):
        pass_copy(k).wait_send()
    for which in range(2):
        for j in range(CHUNKS):
            for stage in range(2):
                for half, d in every:
                    gather(which, j, stage, half, d).wait_send()
    for j in range(CHUNKS):
        keep_copy(j).wait()
        return_copy(j).wait_send()
        remote(res[j].at[odd], out.at[:, :, side(0, j)], o_send.at[j], o_recv.at[j], partner).wait_recv()


def local(coeffs_r, rhs, inverses):
    cycles = coeffs_r.shape[0]
    any_space = pl.BlockSpec(memory_space=pl.ANY)
    dma = pltpu.SemaphoreType.DMA

    def per_chunk(shape, dtype):
        return [pltpu.VMEM((*shape, width), dtype) for width in WIDTHS]

    out = pl.pallas_call(
        kernel,
        out_shape=jax.ShapeDtypeStruct((4, ROWS, 2 * SIDE), BF),
        in_specs=[any_space] * 3,
        out_specs=any_space,
        scratch_shapes=[
            pltpu.VMEM((2, ORDER, ORDER), BF),
            pltpu.VMEM((2, 4, ROWS, SIDE), BF),
            pltpu.VMEM((Z, 8, 2 * ROWS, OWN), BF),
            pltpu.VMEM((2 * ROWS, OWN), BF),
            pltpu.VMEM((2, 8 * ROWS, ORDER), BF),
            pltpu.VMEM((2, Z, HALF, OWN), BF),
            pltpu.VMEM((ROWS, SIDE), BF),
            *per_chunk((Y, X, ROWS), BF),
            *per_chunk((Y, X, ROWS), BF),
            *per_chunk((ORDER,), BF),
            *per_chunk((ORDER,), BF),
            *per_chunk((8 * ROWS,), F32),
            *per_chunk((2, 4, ROWS), BF),
            dma((6 + CHUNKS,)),
            dma((CHUNKS,)),
            dma((CHUNKS, Z - 1)),
            dma((CHUNKS,)),
            dma((Z - 1,)),
            dma,
            dma,
            dma,
            dma((Z - 1,)),
            dma((Z - 1,)),
            dma,
            dma,
            dma((7,)),
            dma((7,)),
            dma((7,)),
            dma((7,)),
            dma((2, CHUNKS, 2, 2, 3)),
            dma((2, CHUNKS, 2, 2, 3)),
            dma((CHUNKS,)),
            dma((CHUNKS,)),
        ],
        compiler_params=pltpu.CompilerParams(
            collective_id=0, has_side_effects=True, vmem_limit_bytes=53 * 1024 * 1024
        ),
    )(
        coeffs_r.reshape(cycles, 2 * ROWS, OWN),
        rhs.reshape(4, ROWS, 2 * SIDE),
        inverses,
    )
    return out.reshape(rhs.shape)


def solution(mesh):
    placed = (P(None, "row", None, None, "col"), P("col", "row", None, "vox"), P())
    return jax.shard_map(
        local, mesh=mesh, in_specs=placed, out_specs=P("col", "row", None, "vox"), check_vma=False
    )
```

```python
import jax
import jax.numpy as jnp
from jax import lax
from jax.experimental import pallas as pl
from jax.experimental.pallas import tpu as pltpu
from jax.sharding import PartitionSpec as P

MESH = pl.DeviceIdType.MESH
BF = jnp.bfloat16
F32 = jnp.float32
X, Y, Z = 4, 4, 8
SIDE = 384
WIDTHS = (256, 128)
STARTS = (0, 256)
CHUNKS = len(WIDTHS)
ROWS = 64
HALF = ROWS // 2
OWN = 128
ORDER = 1024
LAST = Z - 1
FAR_FIRST = (4, 3, 5, 2, 6, 1, 7)
FIRST = (2, 6, 1, 7)


def dot(a, b):
    return jnp.dot(a, b, preferred_element_type=F32)


def picker(rows, wanted):
    r = lax.broadcasted_iota(jnp.int32, (rows, 2 * ROWS), 0)
    c = lax.broadcasted_iota(jnp.int32, (rows, 2 * ROWS), 1)
    return jnp.where(c == wanted(r), 1.0, 0.0).astype(BF)


def kernel(
    coeffs,
    rhs,
    inverses,
    out,
    inv,
    here,
    paired,
    mid_raw,
    factor,
    panel,
    known,
    tail0,
    tail1,
    middle0,
    middle1,
    last0,
    last1,
    solved0,
    solved1,
    acc0,
    acc1,
    res0,
    res1,
    local_sem,
    out_sem,
    t_send,
    t_recv,
    k_send,
    k_recv,
    h_send,
    h_recv,
    p_send,
    p_recv,
    q_send,
    q_recv,
    r_send,
    r_recv,
    s_send,
    s_recv,
    g_send,
    g_recv,
    o_send,
    o_recv,
):
    row = lax.axis_index("row")
    z = lax.axis_index("col")
    core = lax.axis_index("vox")
    x, y = lax.rem(row, X), row // X
    odd = lax.rem(z, 2)
    toward = 1 - 2 * odd
    tail, middle, last = (tail0, tail1), (middle0, middle1), (last0, last1)
    solved_mid, acc, res = (solved0, solved1), (acc0, acc1), (res0, res1)

    def turn(d):
        return lax.rem(z + 2 * Z + d, Z)

    def at_z(d):
        return (row, turn(d), core)

    def at_x(d):
        return (y * X + lax.rem(x + d, X), z, core)

    def at_y(d):
        return (lax.rem(y + d, Y) * X + x, z, core)

    partner = at_z(toward)
    sibling = (row, z, 1 - core)

    def remote(src, dst, send, recv, where):
        return pltpu.make_async_remote_copy(
            src_ref=src, dst_ref=dst, send_sem=send, recv_sem=recv, device_id=where, device_id_type=MESH
        )

    def side(h, j):
        return pl.ds(h * SIDE + STARTS[j], WIDTHS[j])

    my_side = pl.ds(pl.multiple_of(odd * SIDE, OWN), SIDE)
    other_side = pl.ds(pl.multiple_of((1 - odd) * SIDE, OWN), SIDE)
    pair_cycles = 8 * (z // 2)

    load_mid = pltpu.make_async_copy(coeffs.at[30], mid_raw, local_sem.at[0])
    load_inv1 = pltpu.make_async_copy(inverses.at[1], inv.at[1], local_sem.at[1])
    load_own = pltpu.make_async_copy(coeffs.at[pl.ds(pair_cycles, 8)], paired.at[z], local_sem.at[2])
    load_here = pltpu.make_async_copy(rhs.at[:, :, my_side], here.at[odd], local_sem.at[3])
    load_inv0 = pltpu.make_async_copy(inverses.at[0], inv.at[0], local_sem.at[4])
    load_tail = [
        pltpu.make_async_copy(rhs.at[3, :, side(1, j)], tail[j].at[y, x], local_sem.at[5 + j]) for j in range(CHUNKS)
    ]
    load_known = pltpu.make_async_copy(rhs.at[2, :, pl.ds(SIDE, SIDE)], known, local_sem.at[5 + CHUNKS])

    barrier = pltpu.get_barrier_semaphore()
    peers = [at_z(d) for d in range(1, Z)] + [at_x(d) for d in range(1, X)] + [at_y(d) for d in range(1, Y)] + [sibling]
    for peer in peers:
        pl.semaphore_signal(barrier, inc=1, device_id=peer, device_id_type=MESH)
    load_mid.start()

    @pl.when(z == LAST)
    def _():
        for load in (*load_tail, load_known):
            load.start()

    for load in (load_inv1, load_own, load_here, load_inv0):
        load.start()
    load_mid.wait()
    panel[core, z] = dot(picker(HALF, lambda r: 2 * (r + HALF * core) + 1), mid_raw[...]).astype(BF)
    pl.semaphore_wait(barrier, len(peers))

    def tail_copy(j, d):
        return remote(rhs.at[3, :, side((d - 1) % 2, j)], tail[j].at[y, x], t_send.at[j, d - 1], t_recv.at[j], at_z(d))

    def known_copy(d):
        return remote(rhs.at[2, :, pl.ds((d - 1) % 2 * SIDE, SIDE)], known, k_send.at[d - 1], k_recv, at_z(d))

    passes = (z <= 1, z == LAST - 1)
    onward = jnp.where(z <= 1, 2, -2)

    def tail_pass(j):
        return remote(tail[j].at[y, x], tail[j].at[y, x], t_send.at[j, 0], t_recv.at[j], at_z(onward))

    def known_pass():
        return remote(known, known, k_send.at[0], k_recv, at_z(onward))

    def here_copy():
        return remote(rhs.at[:, :, other_side], here.at[odd], h_send, h_recv, partner)

    def panel_copy(d):
        part = panel.at[core, z]
        return remote(part, part, p_send.at[d - 1], p_recv.at[d - 1], at_z(d))

    def panel_share():
        return remote(panel.at[core], panel.at[core], q_send, q_recv, sibling)

    four = pl.ds(4 * core, 4)

    def factor_copy(k):
        shift = {1: -toward, 2: 2 * toward, 3: -3 * toward, 4: toward}[k]
        source = coeffs.at[pl.ds(8 * (turn(shift) // 2) + 4 * core, 4)]
        return remote(source, paired.at[z, four], r_send.at[k - 1], r_recv.at[k - 1], at_z(shift))

    def pass_copy(k):
        part = paired.at[turn(-k * toward), four]
        return remote(part, part, r_send.at[3 + k], r_recv.at[3 + k], partner)

    def share_copy(k):
        part = paired.at[turn(-k * toward if k < 4 else (k - 3) * toward), four]
        return remote(part, part, s_send.at[k - 1], s_recv.at[k - 1], sibling)

    @pl.when(z == LAST)
    def _():
        for j in range(CHUNKS):
            for d in FIRST:
                tail_copy(j, d).start()

    for d in FAR_FIRST:
        panel_copy(d).start()

    @pl.when(z == LAST)
    def _():
        for d in FIRST:
            known_copy(d).start()
        for load in (*load_tail, load_known):
            load.wait()

    for k in (4, 1):
        factor_copy(k).start()

    upper, lower = pl.ds(0, HALF), pl.ds(HALF, HALF)

    def gather(which, j, stage, half, d):
        buf = (tail, middle)[which][j]
        send, recv = g_send.at[which, j, stage, half, d - 1], g_recv.at[which, j, stage, half, d - 1]
        if stage == 0:
            part, where = buf.at[y, x, upper if half == 0 else lower], (at_x(d) if half == 0 else at_y(d))
        elif half == 0:
            part, where = buf.at[y, :, upper], at_y(d)
        else:
            part, where = buf.at[:, x, lower], at_x(d)
        return remote(part, part, send, recv, where)

    every = [(half, d) for d in (2, 1, 3) for half in (0, 1)]

    def start(which, j, stage):
        for half, d in every:
            gather(which, j, stage, half, d).start()

    def arrive(which, j, stage):
        for half, d in every:
            gather(which, j, stage, half, d).wait_recv()

    def step(which, j):
        arrive(which, j, 0)
        start(which, j, 1)

    for j in range(CHUNKS):

        @pl.when(z != LAST)
        def _():
            tail_copy(j, 1).wait_recv()

            @pl.when(jnp.logical_or(*passes))
            def _():
                tail_pass(j).start()

        start(0, j, 0)
    for k in (2, 3):
        factor_copy(k).start()
    here_copy().start()

    step(0, 0)

    @pl.when(jnp.logical_or(*passes))
    def _():
        known_copy(1).wait_recv()
        known_pass().start()

    step(0, 1)

    def relay(k):
        factor_copy(k).wait_recv()
        pass_copy(k).start()
        share_copy(k).start()

    for d in FAR_FIRST:
        panel_copy(d).wait_recv()
    panel_share().start()
    load_inv1.wait()

    @pl.when(jnp.logical_and(z >= 2, z <= LAST - 2))
    def _():
        known_copy(1).wait_recv()

    panel_share().wait_recv()
    panel_full = jnp.concatenate(
        [jnp.concatenate([panel[v, c] for c in range(Z)], axis=1) for v in range(2)], axis=0
    )

    def solve_last(j):
        arrive(0, j, 1)
        solved = dot(inv[1], tail[j][...].reshape(ORDER, WIDTHS[j])).astype(BF)
        last[j][...] = solved
        part = known[:, STARTS[j] : STARTS[j] + WIDTHS[j]].astype(F32) - dot(panel_full, solved)
        middle[j][y, x] = part.astype(BF)
        start(1, j, 0)

    relay(1)
    factor_copy(4).wait_recv()
    share_copy(4).start()
    solve_last(0)
    solve_last(1)
    relay(2)
    relay(3)
    step(1, 0)
    step(1, 1)
    for k in (1, 2, 3):
        pass_copy(k).wait_recv()
        share_copy(4 + k).start()
    load_own.wait()
    load_here.wait()
    here_copy().wait_recv()
    load_inv0.wait()
    for k in range(1, 8):
        share_copy(k).wait_recv()
    pick = picker(2 * ROWS, lambda r: jnp.where(r < ROWS, 2 * r, 2 * (r - ROWS) + 1))
    for k in range(8):
        both = dot(pick, jnp.concatenate([paired[c, k] for c in range(Z)], axis=1)).astype(BF)
        factor[0, k * ROWS : (k + 1) * ROWS] = both[:ROWS]
        factor[1, k * ROWS : (k + 1) * ROWS] = both[ROWS:]
    for j in range(CHUNKS):
        right = here[:, :, :, STARTS[j] : STARTS[j] + WIDTHS[j]].reshape(8 * ROWS, WIDTHS[j]).astype(F32)
        acc[j][...] = right - dot(factor[1], last[j][...])

    own_rows = pl.ds(pl.multiple_of(row * ROWS, ROWS), ROWS)

    def result_place(j):
        return out.at[:, :, pl.ds(pl.multiple_of(odd * SIDE + STARTS[j], OWN), WIDTHS[j])]

    def keep_copy(j):
        return pltpu.make_async_copy(res[j].at[odd], result_place(j), out_sem.at[j])

    def return_copy(j):
        return remote(res[j].at[1 - odd], result_place(j), o_send.at[j], o_recv.at[j], partner)

    for j in range(CHUNKS):
        arrive(1, j, 1)
        solved = dot(inv[0], middle[j][...].reshape(ORDER, WIDTHS[j])).astype(BF)
        solved_mid[j][...] = solved
        result = (acc[j][...] - dot(factor[0], solved)).astype(BF)
        res[j][...] = result.reshape(2, 4, ROWS, WIDTHS[j])

        @pl.when(z >= LAST - 1)
        def _():
            res[j][1, 2] = solved_mid[j][own_rows]
            res[j][1, 3] = last[j][own_rows]

        return_copy(j).start()
        keep_copy(j).start()

    @pl.when(z == LAST)
    def _():
        for d in FIRST:
            for j in range(CHUNKS):
                tail_copy(j, d).wait_send()
            known_copy(d).wait_send()

    @pl.when(jnp.logical_or(*passes))
    def _():
        for j in range(CHUNKS):
            tail_pass(j).wait_send()
        known_pass().wait_send()

    for d in FAR_FIRST:
        panel_copy(d).wait_send()
    panel_share().wait_send()
    here_copy().wait_send()
    for k in range(1, 8):
        share_copy(k).wait_send()
    for k in range(1, 5):
        factor_copy(k).wait_send()
    for k in range(1, 4):
        pass_copy(k).wait_send()
    for which in range(2):
        for j in range(CHUNKS):
            for stage in range(2):
                for half, d in every:
                    gather(which, j, stage, half, d).wait_send()
    for j in range(CHUNKS):
        keep_copy(j).wait()
        return_copy(j).wait_send()
        remote(res[j].at[odd], out.at[:, :, side(0, j)], o_send.at[j], o_recv.at[j], partner).wait_recv()


def local(coeffs_r, rhs, inverses):
    cycles = coeffs_r.shape[0]
    any_space = pl.BlockSpec(memory_space=pl.ANY)
    dma = pltpu.SemaphoreType.DMA

    def per_chunk(shape, dtype):
        return [pltpu.VMEM((*shape, width), dtype) for width in WIDTHS]

    out = pl.pallas_call(
        kernel,
        out_shape=jax.ShapeDtypeStruct((4, ROWS, 2 * SIDE), BF),
        in_specs=[any_space] * 3,
        out_specs=any_space,
        scratch_shapes=[
            pltpu.VMEM((2, ORDER, ORDER), BF),
            pltpu.VMEM((2, 4, ROWS, SIDE), BF),
            pltpu.VMEM((Z, 8, 2 * ROWS, OWN), BF),
            pltpu.VMEM((2 * ROWS, OWN), BF),
            pltpu.VMEM((2, 8 * ROWS, ORDER), BF),
            pltpu.VMEM((2, Z, HALF, OWN), BF),
            pltpu.VMEM((ROWS, SIDE), BF),
            *per_chunk((Y, X, ROWS), BF),
            *per_chunk((Y, X, ROWS), BF),
            *per_chunk((ORDER,), BF),
            *per_chunk((ORDER,), BF),
            *per_chunk((8 * ROWS,), F32),
            *per_chunk((2, 4, ROWS), BF),
            dma((6 + CHUNKS,)),
            dma((CHUNKS,)),
            dma((CHUNKS, Z - 1)),
            dma((CHUNKS,)),
            dma((Z - 1,)),
            dma,
            dma,
            dma,
            dma((Z - 1,)),
            dma((Z - 1,)),
            dma,
            dma,
            dma((7,)),
            dma((7,)),
            dma((7,)),
            dma((7,)),
            dma((2, CHUNKS, 2, 2, 3)),
            dma((2, CHUNKS, 2, 2, 3)),
            dma((CHUNKS,)),
            dma((CHUNKS,)),
        ],
        compiler_params=pltpu.CompilerParams(
            collective_id=0, has_side_effects=True, vmem_limit_bytes=53 * 1024 * 1024
        ),
    )(
        coeffs_r.reshape(cycles, 2 * ROWS, OWN),
        rhs.reshape(4, ROWS, 2 * SIDE),
        inverses,
    )
    return out.reshape(rhs.shape)


def solution(mesh):
    placed = (P(None, "row", None, None, "col"), P("col", "row", None, "vox"), P())
    return jax.shard_map(
        local, mesh=mesh, in_specs=placed, out_specs=P("col", "row", None, "vox"), check_vma=False
    )
```

```python
import jax
import jax.numpy as jnp
from jax import lax
from jax.experimental import pallas as pl
from jax.experimental.pallas import tpu as pltpu
from jax.sharding import PartitionSpec as P

MESH = pl.DeviceIdType.MESH
BF = jnp.bfloat16
F32 = jnp.float32
X, Y, Z = 4, 4, 8
SIDE = 384
WIDTHS = (256, 128)
STARTS = (0, 256)
CHUNKS = len(WIDTHS)
ROWS = 64
HALF = ROWS // 2
OWN = 128
ORDER = 1024
LAST = Z - 1
FAR_FIRST = (4, 3, 5, 2, 6, 1, 7)
FIRST = (2, 6, 1, 7)


def dot(a, b):
    return jnp.dot(a, b, preferred_element_type=F32)


def picker(rows, wanted):
    r = lax.broadcasted_iota(jnp.int32, (rows, 2 * ROWS), 0)
    c = lax.broadcasted_iota(jnp.int32, (rows, 2 * ROWS), 1)
    return jnp.where(c == wanted(r), 1.0, 0.0).astype(BF)


def kernel(
    coeffs,
    rhs,
    inverses,
    out,
    inv,
    here,
    paired,
    mid_raw,
    factor,
    panel,
    known,
    tail0,
    tail1,
    middle0,
    middle1,
    last0,
    last1,
    solved0,
    solved1,
    acc0,
    acc1,
    res0,
    res1,
    local_sem,
    out_sem,
    t_send,
    t_recv,
    k_send,
    k_recv,
    h_send,
    h_recv,
    p_send,
    p_recv,
    q_send,
    q_recv,
    r_send,
    r_recv,
    s_send,
    s_recv,
    g_send,
    g_recv,
    o_send,
    o_recv,
):
    row = lax.axis_index("row")
    z = lax.axis_index("col")
    core = lax.axis_index("vox")
    x, y = lax.rem(row, X), row // X
    odd = lax.rem(z, 2)
    toward = 1 - 2 * odd
    tail, middle, last = (tail0, tail1), (middle0, middle1), (last0, last1)
    solved_mid, acc, res = (solved0, solved1), (acc0, acc1), (res0, res1)

    def turn(d):
        return lax.rem(z + 2 * Z + d, Z)

    def at_z(d):
        return (row, turn(d), core)

    def at_x(d):
        return (y * X + lax.rem(x + d, X), z, core)

    def at_y(d):
        return (lax.rem(y + d, Y) * X + x, z, core)

    partner = at_z(toward)
    sibling = (row, z, 1 - core)

    def remote(src, dst, send, recv, where):
        return pltpu.make_async_remote_copy(
            src_ref=src, dst_ref=dst, send_sem=send, recv_sem=recv, device_id=where, device_id_type=MESH
        )

    def side(h, j):
        return pl.ds(h * SIDE + STARTS[j], WIDTHS[j])

    my_side = pl.ds(pl.multiple_of(odd * SIDE, OWN), SIDE)
    other_side = pl.ds(pl.multiple_of((1 - odd) * SIDE, OWN), SIDE)
    pair_cycles = 8 * (z // 2)

    load_mid = pltpu.make_async_copy(coeffs.at[30], mid_raw, local_sem.at[0])
    load_inv1 = pltpu.make_async_copy(inverses.at[1], inv.at[1], local_sem.at[1])
    load_own = pltpu.make_async_copy(coeffs.at[pl.ds(pair_cycles, 8)], paired.at[z], local_sem.at[2])
    load_here = pltpu.make_async_copy(rhs.at[:, :, my_side], here.at[odd], local_sem.at[3])
    load_inv0 = pltpu.make_async_copy(inverses.at[0], inv.at[0], local_sem.at[4])
    load_tail = [
        pltpu.make_async_copy(rhs.at[3, :, side(1, j)], tail[j].at[y, x], local_sem.at[5 + j]) for j in range(CHUNKS)
    ]
    load_known = pltpu.make_async_copy(rhs.at[2, :, pl.ds(SIDE, SIDE)], known, local_sem.at[5 + CHUNKS])

    barrier = pltpu.get_barrier_semaphore()
    peers = [at_z(d) for d in range(1, Z)] + [at_x(d) for d in range(1, X)] + [at_y(d) for d in range(1, Y)] + [sibling]
    for peer in peers:
        pl.semaphore_signal(barrier, inc=1, device_id=peer, device_id_type=MESH)
    load_mid.start()

    @pl.when(z == LAST)
    def _():
        for load in (*load_tail, load_known):
            load.start()

    for load in (load_inv1, load_own, load_here, load_inv0):
        load.start()
    load_mid.wait()
    panel[core, z] = dot(picker(HALF, lambda r: 2 * (r + HALF * core) + 1), mid_raw[...]).astype(BF)
    pl.semaphore_wait(barrier, len(peers))

    def tail_copy(j, d):
        return remote(rhs.at[3, :, side((d - 1) % 2, j)], tail[j].at[y, x], t_send.at[j, d - 1], t_recv.at[j], at_z(d))

    def known_copy(d):
        return remote(rhs.at[2, :, pl.ds((d - 1) % 2 * SIDE, SIDE)], known, k_send.at[d - 1], k_recv, at_z(d))

    passes = (z <= 1, z == LAST - 1)
    onward = jnp.where(z <= 1, 2, -2)

    def tail_pass(j):
        return remote(tail[j].at[y, x], tail[j].at[y, x], t_send.at[j, 0], t_recv.at[j], at_z(onward))

    def known_pass():
        return remote(known, known, k_send.at[0], k_recv, at_z(onward))

    def here_copy():
        return remote(rhs.at[:, :, other_side], here.at[odd], h_send, h_recv, partner)

    def panel_copy(d):
        part = panel.at[core, z]
        return remote(part, part, p_send.at[d - 1], p_recv.at[d - 1], at_z(d))

    def panel_share():
        return remote(panel.at[core], panel.at[core], q_send, q_recv, sibling)

    four = pl.ds(4 * core, 4)

    def factor_copy(k):
        shift = {1: -toward, 2: 2 * toward, 3: -3 * toward, 4: toward}[k]
        source = coeffs.at[pl.ds(8 * (turn(shift) // 2) + 4 * core, 4)]
        return remote(source, paired.at[z, four], r_send.at[k - 1], r_recv.at[k - 1], at_z(shift))

    def pass_copy(k):
        part = paired.at[turn(-k * toward), four]
        return remote(part, part, r_send.at[3 + k], r_recv.at[3 + k], partner)

    def share_copy(k):
        part = paired.at[turn(-k * toward if k < 4 else (k - 3) * toward), four]
        return remote(part, part, s_send.at[k - 1], s_recv.at[k - 1], sibling)

    @pl.when(z == LAST)
    def _():
        for j in range(CHUNKS):
            for d in FIRST:
                tail_copy(j, d).start()

    for d in FAR_FIRST:
        panel_copy(d).start()

    @pl.when(z == LAST)
    def _():
        for d in FIRST:
            known_copy(d).start()
        for load in (*load_tail, load_known):
            load.wait()

    for k in (4, 1):
        factor_copy(k).start()

    upper, lower = pl.ds(0, HALF), pl.ds(HALF, HALF)

    def gather(which, j, stage, half, d):
        buf = (tail, middle)[which][j]
        send, recv = g_send.at[which, j, stage, half, d - 1], g_recv.at[which, j, stage, half, d - 1]
        if stage == 0:
            part, where = buf.at[y, x, upper if half == 0 else lower], (at_x(d) if half == 0 else at_y(d))
        elif half == 0:
            part, where = buf.at[y, :, upper], at_y(d)
        else:
            part, where = buf.at[:, x, lower], at_x(d)
        return remote(part, part, send, recv, where)

    every = [(half, d) for d in (2, 1, 3) for half in (0, 1)]

    def start(which, j, stage):
        for half, d in every:
            gather(which, j, stage, half, d).start()

    def arrive(which, j, stage):
        for half, d in every:
            gather(which, j, stage, half, d).wait_recv()

    def step(which, j):
        arrive(which, j, 0)
        start(which, j, 1)

    for j in range(CHUNKS):

        @pl.when(z != LAST)
        def _():
            tail_copy(j, 1).wait_recv()

            @pl.when(jnp.logical_or(*passes))
            def _():
                tail_pass(j).start()

        start(0, j, 0)
    for k in (2, 3):
        factor_copy(k).start()
    here_copy().start()

    step(0, 0)

    @pl.when(jnp.logical_or(*passes))
    def _():
        known_copy(1).wait_recv()
        known_pass().start()

    step(0, 1)

    def relay(k):
        factor_copy(k).wait_recv()
        pass_copy(k).start()
        share_copy(k).start()

    for d in FAR_FIRST:
        panel_copy(d).wait_recv()
    panel_share().start()
    load_inv1.wait()


    def solve_last(j):
        arrive(0, j, 1)
        solved = dot(inv[1], tail[j][...].reshape(ORDER, WIDTHS[j])).astype(BF)
        last[j][...] = solved
        if j == 0:

            @pl.when(jnp.logical_and(z >= 2, z <= LAST - 2))
            def _():
                known_copy(1).wait_recv()

            panel_share().wait_recv()
        panel_full = jnp.concatenate(
            [jnp.concatenate([panel[v, c] for c in range(Z)], axis=1) for v in range(2)], axis=0
        )
        part = known[:, STARTS[j] : STARTS[j] + WIDTHS[j]].astype(F32) - dot(panel_full, solved)
        middle[j][y, x] = part.astype(BF)
        start(1, j, 0)

    relay(1)
    factor_copy(4).wait_recv()
    share_copy(4).start()
    solve_last(0)
    solve_last(1)
    relay(2)
    relay(3)
    step(1, 0)
    step(1, 1)
    def prepare():
        for k in (1, 2, 3):
            pass_copy(k).wait_recv()
            share_copy(4 + k).start()
        load_own.wait()
        load_here.wait()
        here_copy().wait_recv()
        for k in range(1, 8):
            share_copy(k).wait_recv()
        pick = picker(2 * ROWS, lambda r: jnp.where(r < ROWS, 2 * r, 2 * (r - ROWS) + 1))
        for k in range(8):
            both = dot(pick, jnp.concatenate([paired[c, k] for c in range(Z)], axis=1)).astype(BF)
            factor[0, k * ROWS : (k + 1) * ROWS] = both[:ROWS]
            factor[1, k * ROWS : (k + 1) * ROWS] = both[ROWS:]
        for j in range(CHUNKS):
            right = here[:, :, :, STARTS[j] : STARTS[j] + WIDTHS[j]].reshape(8 * ROWS, WIDTHS[j]).astype(F32)
            acc[j][...] = right - dot(factor[1], last[j][...])

    def solve_mid(j):
        arrive(1, j, 1)
        solved_mid[j][...] = dot(inv[0], middle[j][...].reshape(ORDER, WIDTHS[j])).astype(BF)

    near = jnp.logical_or(z <= 1, z >= 6)
    load_inv0.wait()

    @pl.when(near)
    def _():
        for j in range(CHUNKS):
            solve_mid(j)

    prepare()

    own_rows = pl.ds(pl.multiple_of(row * ROWS, ROWS), ROWS)

    def result_place(j):
        return out.at[:, :, pl.ds(pl.multiple_of(odd * SIDE + STARTS[j], OWN), WIDTHS[j])]

    def keep_copy(j):
        return pltpu.make_async_copy(res[j].at[odd], result_place(j), out_sem.at[j])

    def return_copy(j):
        return remote(res[j].at[1 - odd], result_place(j), o_send.at[j], o_recv.at[j], partner)

    for j in range(CHUNKS):

        @pl.when(jnp.logical_not(near))
        def _():
            solve_mid(j)

        result = (acc[j][...] - dot(factor[0], solved_mid[j][...])).astype(BF)
        res[j][...] = result.reshape(2, 4, ROWS, WIDTHS[j])

        @pl.when(z >= LAST - 1)
        def _():
            res[j][1, 2] = solved_mid[j][own_rows]
            res[j][1, 3] = last[j][own_rows]

        return_copy(j).start()
        keep_copy(j).start()

    @pl.when(z == LAST)
    def _():
        for d in FIRST:
            for j in range(CHUNKS):
                tail_copy(j, d).wait_send()
            known_copy(d).wait_send()

    @pl.when(jnp.logical_or(*passes))
    def _():
        for j in range(CHUNKS):
            tail_pass(j).wait_send()
        known_pass().wait_send()

    for d in FAR_FIRST:
        panel_copy(d).wait_send()
    panel_share().wait_send()
    here_copy().wait_send()
    for k in range(1, 8):
        share_copy(k).wait_send()
    for k in range(1, 5):
        factor_copy(k).wait_send()
    for k in range(1, 4):
        pass_copy(k).wait_send()
    for which in range(2):
        for j in range(CHUNKS):
            for stage in range(2):
                for half, d in every:
                    gather(which, j, stage, half, d).wait_send()
    for j in range(CHUNKS):
        keep_copy(j).wait()
        return_copy(j).wait_send()
        remote(res[j].at[odd], out.at[:, :, side(0, j)], o_send.at[j], o_recv.at[j], partner).wait_recv()


def local(coeffs_r, rhs, inverses):
    cycles = coeffs_r.shape[0]
    any_space = pl.BlockSpec(memory_space=pl.ANY)
    dma = pltpu.SemaphoreType.DMA

    def per_chunk(shape, dtype):
        return [pltpu.VMEM((*shape, width), dtype) for width in WIDTHS]

    out = pl.pallas_call(
        kernel,
        out_shape=jax.ShapeDtypeStruct((4, ROWS, 2 * SIDE), BF),
        in_specs=[any_space] * 3,
        out_specs=any_space,
        scratch_shapes=[
            pltpu.VMEM((2, ORDER, ORDER), BF),
            pltpu.VMEM((2, 4, ROWS, SIDE), BF),
            pltpu.VMEM((Z, 8, 2 * ROWS, OWN), BF),
            pltpu.VMEM((2 * ROWS, OWN), BF),
            pltpu.VMEM((2, 8 * ROWS, ORDER), BF),
            pltpu.VMEM((2, Z, HALF, OWN), BF),
            pltpu.VMEM((ROWS, SIDE), BF),
            *per_chunk((Y, X, ROWS), BF),
            *per_chunk((Y, X, ROWS), BF),
            *per_chunk((ORDER,), BF),
            *per_chunk((ORDER,), BF),
            *per_chunk((8 * ROWS,), F32),
            *per_chunk((2, 4, ROWS), BF),
            dma((6 + CHUNKS,)),
            dma((CHUNKS,)),
            dma((CHUNKS, Z - 1)),
            dma((CHUNKS,)),
            dma((Z - 1,)),
            dma,
            dma,
            dma,
            dma((Z - 1,)),
            dma((Z - 1,)),
            dma,
            dma,
            dma((7,)),
            dma((7,)),
            dma((7,)),
            dma((7,)),
            dma((2, CHUNKS, 2, 2, 3)),
            dma((2, CHUNKS, 2, 2, 3)),
            dma((CHUNKS,)),
            dma((CHUNKS,)),
        ],
        compiler_params=pltpu.CompilerParams(
            collective_id=0, has_side_effects=True, vmem_limit_bytes=53 * 1024 * 1024
        ),
    )(
        coeffs_r.reshape(cycles, 2 * ROWS, OWN),
        rhs.reshape(4, ROWS, 2 * SIDE),
        inverses,
    )
    return out.reshape(rhs.shape)


def solution(mesh):
    placed = (P(None, "row", None, None, "col"), P("col", "row", None, "vox"), P())
    return jax.shard_map(
        local, mesh=mesh, in_specs=placed, out_specs=P("col", "row", None, "vox"), check_vma=False
    )
```

```python
import jax
import jax.numpy as jnp
from jax import lax
from jax.experimental import pallas as pl
from jax.experimental.pallas import tpu as pltpu
from jax.sharding import PartitionSpec as P

MESH = pl.DeviceIdType.MESH
BF = jnp.bfloat16
F32 = jnp.float32
X, Y, Z = 4, 4, 8
SIDE = 384
WIDTHS = (256, 128)
STARTS = (0, 256)
CHUNKS = len(WIDTHS)
ROWS = 64
HALF = ROWS // 2
OWN = 128
ORDER = 1024
LAST = Z - 1
FAR_FIRST = (4, 3, 5, 2, 6, 1, 7)
FIRST = (2, 6, 1, 7)


def dot(a, b):
    return jnp.dot(a, b, preferred_element_type=F32)


def picker(rows, wanted):
    r = lax.broadcasted_iota(jnp.int32, (rows, 2 * ROWS), 0)
    c = lax.broadcasted_iota(jnp.int32, (rows, 2 * ROWS), 1)
    return jnp.where(c == wanted(r), 1.0, 0.0).astype(BF)


def kernel(
    coeffs,
    rhs,
    inverses,
    out,
    inv,
    here,
    paired,
    mid_raw,
    factor,
    panel,
    known,
    tail0,
    tail1,
    middle0,
    middle1,
    last0,
    last1,
    solved0,
    solved1,
    acc0,
    acc1,
    res0,
    res1,
    local_sem,
    out_sem,
    t_send,
    t_recv,
    k_send,
    k_recv,
    h_send,
    h_recv,
    p_send,
    p_recv,
    q_send,
    q_recv,
    r_send,
    r_recv,
    s_send,
    s_recv,
    g_send,
    g_recv,
    o_send,
    o_recv,
):
    row = lax.axis_index("row")
    z = lax.axis_index("col")
    core = lax.axis_index("vox")
    x, y = lax.rem(row, X), row // X
    odd = lax.rem(z, 2)
    toward = 1 - 2 * odd
    tail, middle, last = (tail0, tail1), (middle0, middle1), (last0, last1)
    solved_mid, acc, res = (solved0, solved1), (acc0, acc1), (res0, res1)

    def turn(d):
        return lax.rem(z + 2 * Z + d, Z)

    def at_z(d):
        return (row, turn(d), core)

    def at_x(d):
        return (y * X + lax.rem(x + d, X), z, core)

    def at_y(d):
        return (lax.rem(y + d, Y) * X + x, z, core)

    partner = at_z(toward)
    sibling = (row, z, 1 - core)

    def remote(src, dst, send, recv, where):
        return pltpu.make_async_remote_copy(
            src_ref=src, dst_ref=dst, send_sem=send, recv_sem=recv, device_id=where, device_id_type=MESH
        )

    def side(h, j):
        return pl.ds(h * SIDE + STARTS[j], WIDTHS[j])

    my_side = pl.ds(pl.multiple_of(odd * SIDE, OWN), SIDE)
    other_side = pl.ds(pl.multiple_of((1 - odd) * SIDE, OWN), SIDE)
    pair_cycles = 8 * (z // 2)

    load_mid = pltpu.make_async_copy(coeffs.at[30], mid_raw, local_sem.at[0])
    load_inv1 = pltpu.make_async_copy(inverses.at[1], inv.at[1], local_sem.at[1])
    load_own = pltpu.make_async_copy(coeffs.at[pl.ds(pair_cycles, 8)], paired.at[z], local_sem.at[2])
    load_here = pltpu.make_async_copy(rhs.at[:, :, my_side], here.at[odd], local_sem.at[3])
    load_inv0 = pltpu.make_async_copy(inverses.at[0], inv.at[0], local_sem.at[4])
    load_tail = [
        pltpu.make_async_copy(rhs.at[3, :, side(1, j)], tail[j].at[y, x], local_sem.at[5 + j]) for j in range(CHUNKS)
    ]
    load_known = pltpu.make_async_copy(rhs.at[2, :, pl.ds(SIDE, SIDE)], known, local_sem.at[5 + CHUNKS])

    barrier = pltpu.get_barrier_semaphore()
    peers = [at_z(d) for d in range(1, Z)] + [at_x(d) for d in range(1, X)] + [at_y(d) for d in range(1, Y)] + [sibling]
    for peer in peers:
        pl.semaphore_signal(barrier, inc=1, device_id=peer, device_id_type=MESH)
    load_mid.start()

    @pl.when(z == LAST)
    def _():
        for load in (*load_tail, load_known):
            load.start()

    for load in (load_inv1, load_own, load_here, load_inv0):
        load.start()
    load_mid.wait()
    panel[core, z] = dot(picker(HALF, lambda r: 2 * (r + HALF * core) + 1), mid_raw[...]).astype(BF)
    pl.semaphore_wait(barrier, len(peers))

    def tail_copy(j, d):
        return remote(rhs.at[3, :, side((d - 1) % 2, j)], tail[j].at[y, x], t_send.at[j, d - 1], t_recv.at[j], at_z(d))

    def known_copy(d):
        return remote(rhs.at[2, :, pl.ds((d - 1) % 2 * SIDE, SIDE)], known, k_send.at[d - 1], k_recv, at_z(d))

    passes = (z <= 1, z == LAST - 1)
    onward = jnp.where(z <= 1, 2, -2)

    def tail_pass(j):
        return remote(tail[j].at[y, x], tail[j].at[y, x], t_send.at[j, 0], t_recv.at[j], at_z(onward))

    def known_pass():
        return remote(known, known, k_send.at[0], k_recv, at_z(onward))

    def here_copy():
        return remote(rhs.at[:, :, other_side], here.at[odd], h_send, h_recv, partner)

    def panel_copy(d):
        part = panel.at[core, z]
        return remote(part, part, p_send.at[d - 1], p_recv.at[d - 1], at_z(d))

    def panel_share():
        return remote(panel.at[core], panel.at[core], q_send, q_recv, sibling)

    four = pl.ds(4 * core, 4)

    def factor_copy(k):
        shift = {1: -toward, 2: 2 * toward, 3: -3 * toward, 4: toward}[k]
        source = coeffs.at[pl.ds(8 * (turn(shift) // 2) + 4 * core, 4)]
        return remote(source, paired.at[z, four], r_send.at[k - 1], r_recv.at[k - 1], at_z(shift))

    def pass_copy(k):
        part = paired.at[turn(-k * toward), four]
        return remote(part, part, r_send.at[3 + k], r_recv.at[3 + k], partner)

    def share_copy(k):
        part = paired.at[turn(-k * toward if k < 4 else (k - 3) * toward), four]
        return remote(part, part, s_send.at[k - 1], s_recv.at[k - 1], sibling)

    @pl.when(z == LAST)
    def _():
        for j in range(CHUNKS):
            for d in FIRST:
                tail_copy(j, d).start()

    for d in FAR_FIRST:
        panel_copy(d).start()

    @pl.when(z == LAST)
    def _():
        for d in FIRST:
            known_copy(d).start()
        for load in (*load_tail, load_known):
            load.wait()

    for k in (1, 4):
        factor_copy(k).start()
    ahead = {2: z == 6, 3: z == 5}
    for k in (2, 3):

        @pl.when(ahead[k])
        def _():
            factor_copy(k).start()


    upper, lower = pl.ds(0, HALF), pl.ds(HALF, HALF)

    def gather(which, j, stage, half, d):
        buf = (tail, middle)[which][j]
        send, recv = g_send.at[which, j, stage, half, d - 1], g_recv.at[which, j, stage, half, d - 1]
        if stage == 0:
            part, where = buf.at[y, x, upper if half == 0 else lower], (at_x(d) if half == 0 else at_y(d))
        elif half == 0:
            part, where = buf.at[y, :, upper], at_y(d)
        else:
            part, where = buf.at[:, x, lower], at_x(d)
        return remote(part, part, send, recv, where)

    every = [(half, d) for d in (2, 1, 3) for half in (0, 1)]

    def start(which, j, stage):
        for half, d in every:
            gather(which, j, stage, half, d).start()

    def arrive(which, j, stage):
        for half, d in every:
            gather(which, j, stage, half, d).wait_recv()

    def step(which, j):
        arrive(which, j, 0)
        start(which, j, 1)

    for j in range(CHUNKS):

        @pl.when(z != LAST)
        def _():
            tail_copy(j, 1).wait_recv()

            @pl.when(jnp.logical_or(*passes))
            def _():
                tail_pass(j).start()

        start(0, j, 0)
    for k in (3, 2):

        @pl.when(jnp.logical_not(ahead[k]))
        def _():
            factor_copy(k).start()

    here_copy().start()

    step(0, 0)

    @pl.when(jnp.logical_or(*passes))
    def _():
        known_copy(1).wait_recv()
        known_pass().start()

    step(0, 1)

    def relay(k):
        factor_copy(k).wait_recv()
        pass_copy(k).start()
        share_copy(k).start()

    for d in FAR_FIRST:
        panel_copy(d).wait_recv()
    panel_share().start()
    load_inv1.wait()


    def solve_last(j):
        arrive(0, j, 1)
        solved = dot(inv[1], tail[j][...].reshape(ORDER, WIDTHS[j])).astype(BF)
        last[j][...] = solved
        if j == 0:

            @pl.when(jnp.logical_and(z >= 2, z <= LAST - 2))
            def _():
                known_copy(1).wait_recv()

            panel_share().wait_recv()
        panel_full = jnp.concatenate(
            [jnp.concatenate([panel[v, c] for c in range(Z)], axis=1) for v in range(2)], axis=0
        )
        part = known[:, STARTS[j] : STARTS[j] + WIDTHS[j]].astype(F32) - dot(panel_full, solved)
        middle[j][y, x] = part.astype(BF)
        start(1, j, 0)

    relay(1)
    factor_copy(4).wait_recv()
    share_copy(4).start()
    solve_last(0)
    solve_last(1)
    relay(2)
    relay(3)
    step(1, 0)
    step(1, 1)
    def prepare():
        for k in (1, 2, 3):
            pass_copy(k).wait_recv()
            share_copy(4 + k).start()
        load_own.wait()
        load_here.wait()
        here_copy().wait_recv()
        for k in range(1, 8):
            share_copy(k).wait_recv()
        pick = picker(2 * ROWS, lambda r: jnp.where(r < ROWS, 2 * r, 2 * (r - ROWS) + 1))
        for k in range(8):
            both = dot(pick, jnp.concatenate([paired[c, k] for c in range(Z)], axis=1)).astype(BF)
            factor[0, k * ROWS : (k + 1) * ROWS] = both[:ROWS]
            factor[1, k * ROWS : (k + 1) * ROWS] = both[ROWS:]
        for j in range(CHUNKS):
            right = here[:, :, :, STARTS[j] : STARTS[j] + WIDTHS[j]].reshape(8 * ROWS, WIDTHS[j]).astype(F32)
            acc[j][...] = right - dot(factor[1], last[j][...])

    def solve_mid(j):
        arrive(1, j, 1)
        solved_mid[j][...] = dot(inv[0], middle[j][...].reshape(ORDER, WIDTHS[j])).astype(BF)

    near = jnp.logical_or(z <= 1, z >= 6)
    load_inv0.wait()

    @pl.when(near)
    def _():
        for j in range(CHUNKS):
            solve_mid(j)

    prepare()

    own_rows = pl.ds(pl.multiple_of(row * ROWS, ROWS), ROWS)

    def result_place(j):
        return out.at[:, :, pl.ds(pl.multiple_of(odd * SIDE + STARTS[j], OWN), WIDTHS[j])]

    def keep_copy(j):
        return pltpu.make_async_copy(res[j].at[odd], result_place(j), out_sem.at[j])

    def return_copy(j):
        return remote(res[j].at[1 - odd], result_place(j), o_send.at[j], o_recv.at[j], partner)

    for j in range(CHUNKS):

        @pl.when(jnp.logical_not(near))
        def _():
            solve_mid(j)

        result = (acc[j][...] - dot(factor[0], solved_mid[j][...])).astype(BF)
        res[j][...] = result.reshape(2, 4, ROWS, WIDTHS[j])

        @pl.when(z >= LAST - 1)
        def _():
            res[j][1, 2] = solved_mid[j][own_rows]
            res[j][1, 3] = last[j][own_rows]

        return_copy(j).start()
        keep_copy(j).start()

    @pl.when(z == LAST)
    def _():
        for d in FIRST:
            for j in range(CHUNKS):
                tail_copy(j, d).wait_send()
            known_copy(d).wait_send()

    @pl.when(jnp.logical_or(*passes))
    def _():
        for j in range(CHUNKS):
            tail_pass(j).wait_send()
        known_pass().wait_send()

    for d in FAR_FIRST:
        panel_copy(d).wait_send()
    panel_share().wait_send()
    here_copy().wait_send()
    for k in range(1, 8):
        share_copy(k).wait_send()
    for k in range(1, 5):
        factor_copy(k).wait_send()
    for k in range(1, 4):
        pass_copy(k).wait_send()
    for which in range(2):
        for j in range(CHUNKS):
            for stage in range(2):
                for half, d in every:
                    gather(which, j, stage, half, d).wait_send()
    for j in range(CHUNKS):
        keep_copy(j).wait()
        return_copy(j).wait_send()
        remote(res[j].at[odd], out.at[:, :, side(0, j)], o_send.at[j], o_recv.at[j], partner).wait_recv()


def local(coeffs_r, rhs, inverses):
    cycles = coeffs_r.shape[0]
    any_space = pl.BlockSpec(memory_space=pl.ANY)
    dma = pltpu.SemaphoreType.DMA

    def per_chunk(shape, dtype):
        return [pltpu.VMEM((*shape, width), dtype) for width in WIDTHS]

    out = pl.pallas_call(
        kernel,
        out_shape=jax.ShapeDtypeStruct((4, ROWS, 2 * SIDE), BF),
        in_specs=[any_space] * 3,
        out_specs=any_space,
        scratch_shapes=[
            pltpu.VMEM((2, ORDER, ORDER), BF),
            pltpu.VMEM((2, 4, ROWS, SIDE), BF),
            pltpu.VMEM((Z, 8, 2 * ROWS, OWN), BF),
            pltpu.VMEM((2 * ROWS, OWN), BF),
            pltpu.VMEM((2, 8 * ROWS, ORDER), BF),
            pltpu.VMEM((2, Z, HALF, OWN), BF),
            pltpu.VMEM((ROWS, SIDE), BF),
            *per_chunk((Y, X, ROWS), BF),
            *per_chunk((Y, X, ROWS), BF),
            *per_chunk((ORDER,), BF),
            *per_chunk((ORDER,), BF),
            *per_chunk((8 * ROWS,), F32),
            *per_chunk((2, 4, ROWS), BF),
            dma((6 + CHUNKS,)),
            dma((CHUNKS,)),
            dma((CHUNKS, Z - 1)),
            dma((CHUNKS,)),
            dma((Z - 1,)),
            dma,
            dma,
            dma,
            dma((Z - 1,)),
            dma((Z - 1,)),
            dma,
            dma,
            dma((7,)),
            dma((7,)),
            dma((7,)),
            dma((7,)),
            dma((2, CHUNKS, 2, 2, 3)),
            dma((2, CHUNKS, 2, 2, 3)),
            dma((CHUNKS,)),
            dma((CHUNKS,)),
        ],
        compiler_params=pltpu.CompilerParams(
            collective_id=0, has_side_effects=True, vmem_limit_bytes=53 * 1024 * 1024
        ),
    )(
        coeffs_r.reshape(cycles, 2 * ROWS, OWN),
        rhs.reshape(4, ROWS, 2 * SIDE),
        inverses,
    )
    return out.reshape(rhs.shape)


def solution(mesh):
    placed = (P(None, "row", None, None, "col"), P("col", "row", None, "vox"), P())
    return jax.shard_map(
        local, mesh=mesh, in_specs=placed, out_specs=P("col", "row", None, "vox"), check_vma=False
    )
```
